256 devices in a mesh: rep: 2 (over core), expert: 128 (over y, z, x).
Axes of the slice: x: 4, y: 4, z: 8, core: 2. Of those that a mesh axis runs over, the one named last changes fastest.
Arguments:
- tokens: bfloat16 [2048, 3584], P('expert'), may hold values from -6 to 6
- expert_ids: int32 [2048, 8], P('expert'), may hold values from 0 to 127, all different within a row; in each aligned block of 16 rows (0 to 15, 16 to 31, ...) at most 2 rows name the same one
- gate_scores: float32 [2048, 8], P('expert'), may hold values from 0.05 to 1
- w_gate: bfloat16 [128, 3584, 1024], P('expert', None, 'rep'), may hold values from -0.09375 to 0.09375
- w_up: bfloat16 [128, 3584, 1024], P('expert', None, 'rep'), may hold values from -0.09375 to 0.09375
- w_down: bfloat16 [128, 1024, 3584], P('expert', 'rep'), may hold values from -0.1875 to 0.1875
Outputs:
- combined: bfloat16 [2048, 3584], P('expert', 'rep')
The draws below stay inside these ranges and needn't reach their ends.
Inputs may be any that keep to these rules, and one draw needn't show every extreme that they name: `expert_ids`: each row names 8 different experts; within the rows of one device no expert is named by more than 2 rows, a bound that some block reaches.
All inputs are finite; a program needn't handle non-finite values.
Results may differ from the reference program's by a relative error of at most 0.0057.
Values may be sent and summed in bfloat16 or wider, within the bound.
A program may use at most 64 MiB of HBM per device.

```python
import math
import jax
import jax.numpy as jnp
import numpy as np
from jax import lax

D = 3584
H = 1024
K = 8
TOK_DEV = 16
EXPERTS = 128
TOKENS = 2048
CAP = 2
N_EXPERT = 128


def level_of(stream_key, dims, shards, least, top_value):
    loudness = 1.0
    for axis_at, blocks in shards:
        heights = jax.random.uniform(jax.random.fold_in(jax.random.fold_in(stream_key, 6), axis_at), (blocks,), jnp.float32, least / len(shards), top_value / len(shards))
        loudness = loudness * jnp.repeat(jnp.exp(heights), dims[axis_at] // blocks).reshape((-1,) + (1,) * (len(dims) - 1 - axis_at))
    return loudness


def assign_block(rng, own, number, rows, number_of, top, most, lean):
    ranking = jax.random.permutation(rng, number_of)
    packed, usual = portions_of(number_of, rows * top, most, lean, True), portions_of(number_of, rows * top, most, lean, False)
    places = jnp.arange(number_of)

    def named(sizes, offset_by):
        used = int((sizes > 0).sum())
        fixed = max(1, used // 4)
        passed = fixed + (places - fixed + offset_by * (used - fixed)) % max(1, number_of - fixed)
        return jnp.zeros((number_of,), jnp.int32).at[ranking[jnp.where(places < fixed, places, passed)]].set(jnp.asarray(sizes, jnp.int32))

    sizes = jnp.where(number % 4 == 0, named(packed, number // 4), named(usual, number - number // 4 - 1))
    mixed = jax.random.permutation(jax.random.fold_in(own, 3), number_of)
    source_of, sink = mixed[0:number_of // 2 * 2:2], mixed[1:number_of // 2 * 2:2]
    margin = jnp.minimum(sizes[source_of] - 1, most - sizes[sink]) // 2
    margin = jnp.where((source_of == ranking[0]) | (sink == ranking[0]) | (sizes[sink] == 0), 0, jnp.maximum(margin, 0))
    passed = jax.random.randint(jax.random.fold_in(own, 4), (number_of // 2,), 0, 1 << 20) % (margin + 1)
    sizes = sizes.at[source_of].add(-passed).at[sink].add(passed)
    labels = jnp.searchsorted(jnp.cumsum(sizes), jnp.arange(rows * top), side="right").astype(jnp.int32)
    table = labels.reshape(top, rows).T
    table = table[jax.random.permutation(jax.random.fold_in(own, 1), rows)]
    offset_by = jax.random.randint(jax.random.fold_in(own, 2), (rows, 1), 0, top)
    return jnp.take_along_axis(table, (jnp.arange(top)[None, :] + offset_by) % top, axis=1)


def portions_of(number_of, total, limit, lean, full):
    weights = [(1 << 20) // math.isqrt(grade ** lean) + 1 for grade in range(1, number_of + 1)]
    largest = limit if full else min(limit, max(-(-total // number_of), total * weights[0] // sum(weights)))
    least = 1 if total - largest >= number_of - 1 else 0
    counts, surplus = [largest] + [least] * (number_of - 1), total - largest - least * (number_of - 1)
    while surplus > 0:
        candidates = [i for i in range(1, number_of) if counts[i] < largest] or [i for i in range(1, number_of) if counts[i] < limit]
        mass, left = sum([weights[i] for i in candidates]), surplus
        for i in candidates:
            extra = min(limit - counts[i], max(1, left * weights[i] // mass), surplus)
            counts[i] = counts[i] + extra
            surplus = surplus - extra
    return np.array(counts)


def normal_values(own_key, shape, width, bound, shards=(), kind=jnp.bfloat16):
    array = jax.random.normal(own_key, shape, jnp.float32) * width
    if len(shards) > 0:
        array = level_of(own_key, shape, shards, -0.22, 0.18) * array
    return jnp.clip(array, min=-bound, max=bound).astype(kind)


def setup_inputs(seed: int = 0) -> dict:
    keys = jax.random.split(jax.random.key(seed), 7)
    tokens = normal_values(keys[0], (TOKENS, D), 1.0, 6.0, ((0, 128),))
    expert_ids_keys = jax.random.split(jax.random.fold_in(keys[1], 1), TOKENS // TOK_DEV)
    expert_ids_turns = jax.random.permutation(jax.random.fold_in(keys[1], 3), TOKENS // TOK_DEV)
    expert_ids = jax.vmap(lambda own, number: assign_block(jax.random.fold_in(keys[1], 2), own, number, TOK_DEV, EXPERTS, K, CAP, 2))(expert_ids_keys, expert_ids_turns).reshape((TOKENS, K))
    gate_scores = jnp.clip(jnp.exp(math.log(1.0) - 2.9957323 * jax.random.uniform(keys[2], (TOKENS, K), jnp.float32) ** level_of(keys[2], (TOKENS, K), ((0, 128),), -0.2, 0.2)), 0.05, 1.0)
    w_gate = normal_values(keys[3], (EXPERTS, D, H), D ** -0.5, 0.09375, ((0, 128), (2, 2)))
    w_up = normal_values(keys[4], (EXPERTS, D, H), D ** -0.5, 0.09375, ((0, 128), (2, 2)))
    w_down = normal_values(keys[5], (EXPERTS, H, D), H ** -0.5, 0.1875, ((0, 128), (1, 2)))
    return {"tokens": tokens, "expert_ids": expert_ids, "gate_scores": gate_scores, "w_gate": w_gate, "w_up": w_up, "w_down": w_down}


def reference(tokens, expert_ids, gate_scores, w_gate, w_up, w_down):
    token_count = tokens.shape[0]
    flat_ids = expert_ids.reshape(-1).astype(jnp.int32)
    assignments = flat_ids.shape[0]
    one_hot = (flat_ids[:, None] == jnp.arange(EXPERTS, dtype=jnp.int32)[None, :]).astype(jnp.int32)
    blocks = one_hot.reshape(N_EXPERT, TOK_DEV * K, EXPERTS)
    row_rank = (jnp.sum(jnp.cumsum(blocks, 1) * blocks, 2) - 1).reshape(-1).astype(jnp.int32)
    source = jnp.arange(assignments, dtype=jnp.int32) // (TOK_DEV * K)
    slot_index = source * CAP + row_rank
    token_index = jnp.arange(assignments, dtype=jnp.int32) // K
    row_table = jnp.full((EXPERTS, N_EXPERT * CAP), token_count, jnp.int32).at[flat_ids, slot_index].set(token_index)
    scale_table = jnp.zeros((EXPERTS, N_EXPERT * CAP), jnp.float32).at[flat_ids, slot_index].set(gate_scores.reshape(-1).astype(jnp.float32))
    padded = jnp.concatenate([tokens, jnp.zeros((1, D), tokens.dtype)], 0)

    def expert_step(accumulated, pieces):
        row_index, row_scales, gate_weight, up_weight, down_weight = pieces
        block_rows = padded[row_index]
        gate_proj = jnp.dot(block_rows, gate_weight, preferred_element_type=jnp.float32)
        up_proj = jnp.dot(block_rows, up_weight, preferred_element_type=jnp.float32)
        hidden = (jax.nn.silu(gate_proj) * up_proj).astype(jnp.bfloat16)
        expert_out = jnp.dot(hidden, down_weight, preferred_element_type=jnp.float32).astype(jnp.bfloat16)
        accumulated = accumulated.at[row_index].add(expert_out.astype(jnp.float32) * row_scales[:, None], mode="drop")
        return accumulated, None

    accumulated, _ = lax.scan(expert_step, jnp.zeros((token_count, D), jnp.float32), (row_table, scale_table, w_gate, w_up, w_down))
    return accumulated.astype(jnp.bfloat16)
```

```python
import functools

import jax
import jax.numpy as jnp
from jax import lax
from jax.experimental import pallas as pl
from jax.experimental.pallas import tpu as pltpu
from jax.sharding import PartitionSpec as P

NX, NY, NZ = 4, 4, 8
ROWS = 16
TOP = 8
CAP = 2
HALF = 1792
HID = 512
SLOTS = NX * NY * NZ * CAP
COLUMN = NZ * ROWS
CHUNKS_IN = (256, 512, 512, 512)
CHUNKS_OUT = (512, 512, 512, 256)
BF = jnp.bfloat16
F32 = jnp.float32


def starts(widths):
    return [sum(widths[:i]) for i in range(len(widths))]


def dot(lhs, rhs):
    return jnp.dot(lhs, rhs, preferred_element_type=F32)


def kernel(tok, ids, sc, wg, wu, wd, out, *scratch):
    names = iter(scratch)
    n_in, n_out = len(CHUNKS_IN), len(CHUNKS_OUT)
    take = lambda n: [next(names) for _ in range(n)]
    zbuf, send, recv1, recv2, sib = (take(n_in) for _ in range(5))
    outb, ret1, ret2, zsend, zrecv, own = (take(n_out) for _ in range(6))
    ids_v, sc_v, meta, sel_t, w_hi, w_lo, hid, hid_sib, acc_g, acc_u = take(10)
    wg_v, wu_v, wd_own, wd_sib = take(4)
    local, send_sem, recv_sem = take(3)

    r = lax.axis_index("rep")
    e = lax.axis_index("expert")
    y, z, x = e // 32, (e // 4) % 8, e % 4
    a = x * (1 - r) + y * r
    b = y * (1 - r) + x * r

    def device(a_at, b_at, z_at, r_at=r):
        y_at = b_at * (1 - r) + a_at * r
        x_at = a_at * (1 - r) + b_at * r
        return {"rep": r_at, "expert": (y_at * 8 + z_at) * 4 + x_at}

    def along_a(step):
        return device((a + step + 4) % 4, b, z)

    def along_b(step):
        return device(a, (b + step + 4) % 4, z)

    def along_z(step):
        return device(a, b, (z + step + 8) % 8)

    sibling = device(a, b, z, 1 - r)

    index = {}

    def sem_of(key):
        return index.setdefault(key, len(index))

    def push(src, dst, key, target):
        at = sem_of(key)
        pltpu.make_async_remote_copy(
            src_ref=src,
            dst_ref=dst,
            send_sem=send_sem.at[at],
            recv_sem=recv_sem.at[at],
            device_id=target,
        ).start()

    def whole(ref, key):
        at = sem_of(key)
        return pltpu.make_async_remote_copy(
            src_ref=ref,
            dst_ref=ref,
            send_sem=send_sem.at[at],
            recv_sem=recv_sem.at[at],
            device_id=sibling,
        )

    sent = []

    def arrived(ref, key):
        whole(ref, key).wait_recv()
        sent.append((ref, key))

    in_at, out_at = starts(CHUNKS_IN), starts(CHUNKS_OUT)
    mine, other = r * HALF, (1 - r) * HALF

    loads = {}

    def load(name, src, dst):
        loads[name] = pltpu.make_async_copy(src, dst, local.at[len(loads)])
        loads[name].start()

    load("ids", ids, ids_v)
    load("sc", sc, sc_v)
    for c, width in enumerate(CHUNKS_IN):
        load(("tok", c), tok.at[:, pl.ds(pl.multiple_of(mine + in_at[c], 128), width)], zbuf[c].at[0])
    for half, base in ((0, mine), (1, other)):
        rows = pl.ds(pl.multiple_of(base, 128), HALF)
        load(("wg", half), wg.at[0, rows, :], wg_v.at[half])
        load(("wu", half), wu.at[0, rows, :], wu_v.at[half])
    load("wd", wd.at[0, :, pl.ds(pl.multiple_of(mine, 128), HALF)], wd_own)

    barrier = pltpu.get_barrier_semaphore()
    for step in range(1, NZ):
        pl.semaphore_signal(barrier, inc=1, device_id=along_z(step))
    for step in range(1, 4):
        pl.semaphore_signal(barrier, inc=1, device_id=along_a(step))
        pl.semaphore_signal(barrier, inc=1, device_id=along_b(step))
    pl.semaphore_signal(barrier, inc=1, device_id=sibling)

    loads["ids"].wait()
    loads["sc"].wait()
    meta[0, 0:ROWS, 0:TOP] = ids_v[...].astype(F32).T
    meta[0, ROWS:, 0:TOP] = sc_v[...].T
    for c in range(n_in):
        loads["tok", c].wait()
    pl.semaphore_wait(barrier, NZ - 1 + 3 + 3 + 1)

    for step in range(1, NZ):
        push(meta.at[0], meta.at[step], "meta", along_z(step))
    for c in range(n_in):
        for step in range(1, NZ):
            push(zbuf[c].at[0], zbuf[c].at[step], ("z", c), along_z(step))
    push(wd.at[0, :, pl.ds(pl.multiple_of(other, 128), HALF)], wd_sib, "wd", sibling)

    arrived(meta.at[pl.ds(1, NZ - 1)], "meta")
    lane = lax.broadcasted_iota(jnp.int32, (COLUMN, SLOTS), 1)
    row = lax.broadcasted_iota(jnp.int32, (COLUMN, SLOTS), 0)
    a_to = (a + (lane >> 6)) & 3
    b_to = (b + ((lane >> 4) & 3)) & 3
    y_to = b_to * (1 - r) + a_to * r
    x_to = a_to * (1 - r) + b_to * r
    named = ((y_to * 8 + z) * 4 + x_to).astype(F32)
    same = ((lane >> 1) & 7) == (row >> 4)
    ids_all = meta[:, 0:ROWS, :].reshape(COLUMN, 128)
    sc_all = meta[:, ROWS:, :].reshape(COLUMN, 128)
    member = jnp.zeros((COLUMN, SLOTS), F32)
    weight = jnp.zeros((COLUMN, SLOTS), F32)
    for k in range(TOP):
        hit = (ids_all[:, k : k + 1] == named) & same
        member = jnp.where(hit, 1.0, member)
        weight = jnp.where(hit, sc_all[:, k : k + 1], weight)
    to_row = lax.broadcasted_iota(jnp.int32, (COLUMN, COLUMN), 0)
    from_row = lax.broadcasted_iota(jnp.int32, (COLUMN, COLUMN), 1)
    before = jnp.where(((to_row >> 4) == (from_row >> 4)) & (from_row < to_row), 1.0, 0.0)
    rank = dot(before.astype(BF), member.astype(BF))
    chosen = rank == (lane & 1).astype(F32)
    weight = jnp.where(chosen, weight, 0.0)
    high = weight.astype(BF)
    w_hi[...] = high
    w_lo[...] = (weight - high.astype(F32)).astype(BF)
    sel_t[...] = jnp.where(chosen, member, 0.0).T.astype(BF)

    def select(c):
        width = CHUNKS_IN[c]
        arrived(zbuf[c].at[pl.ds(1, NZ - 1)], ("z", c))
        slots = dot(sel_t[...], zbuf[c][...].reshape(COLUMN, width)).astype(BF)
        slots = slots.reshape(4, 4, ROWS, width)
        recv1[c][0] = slots[0]
        send[c][...] = slots[1:]
        for step in range(1, 4):
            push(send[c].at[step - 1], recv1[c].at[step], ("a", c), along_a(step))

    def turn(c):
        arrived(recv1[c].at[pl.ds(1, 3)], ("a", c))
        for step in range(1, 4):
            push(recv1[c].at[:, step], recv2[c].at[step - 1], ("b", c, step), along_b(step))
        push(recv1[c].at[:, 0], sib[c].at[:, 0], ("s", c), sibling)

    def accumulate(block, half, c, first):
        rows = pl.ds(in_at[c], CHUNKS_IN[c])
        gate = dot(block, wg_v[half, rows, :])
        up = dot(block, wu_v[half, rows, :])
        if first:
            acc_g[...] = gate
            acc_u[...] = up
        else:
            acc_g[...] += gate
            acc_u[...] += up

    def landed(c):
        for step in range(1, 4):
            arrived(recv2[c].at[step - 1], ("b", c, step))
            push(recv2[c].at[step - 1], sib[c].at[:, step], ("s", c), sibling)
        if c == 0:
            loads["wg", 0].wait()
            loads["wu", 0].wait()
        width = CHUNKS_IN[c]
        block = jnp.concatenate(
            [recv1[c][:, 0].reshape(4 * ROWS, width), recv2[c][...].reshape(12 * ROWS, width)], 0
        )
        accumulate(block, 0, c, c == 0)

    def siblings(c):
        arrived(sib[c], ("s", c))
        if c == 0:
            loads["wg", 1].wait()
            loads["wu", 1].wait()
        accumulate(sib[c][...].reshape(SLOTS, CHUNKS_IN[c]), 1, c, False)

    for tick in range(n_in + 3):
        for stage, lag in ((select, 0), (turn, 1), (landed, 2), (siblings, 3)):
            if 0 <= tick - lag < n_in:
                stage(tick - lag)

    gate = acc_g[...]
    hid[...] = (gate / (1.0 + jnp.exp(-gate)) * acc_u[...]).astype(BF).reshape(4, 4, ROWS, HID)
    for step in range(4):
        push(hid.at[step], hid_sib.at[:, step], "hid", sibling)
    loads["wd"].wait()
    arrived(wd_sib, "wd")

    def down(c):
        width = CHUNKS_OUT[c]
        columns = pl.ds(out_at[c], width)
        total = dot(hid[...].reshape(SLOTS, HID), wd_own[:, columns])
        if c == 0:
            arrived(hid_sib, "hid")
        total = total + dot(hid_sib[...].reshape(SLOTS, HID), wd_sib[:, columns])
        blocks = total.astype(BF).reshape(4, 4, ROWS, width)
        ret1[c][0] = blocks[0]
        outb[c][...] = blocks[1:]
        for step in range(1, 4):
            push(outb[c].at[step - 1], ret1[c].at[step], ("rb", c), along_b(-step))

    def turn_back(c):
        arrived(ret1[c].at[pl.ds(1, 3)], ("rb", c))
        for step in range(1, 4):
            push(ret1[c].at[:, step], ret2[c].at[step - 1], ("ra", c), along_a(-step))

    def combine(c):
        width = CHUNKS_OUT[c]
        arrived(ret2[c], ("ra", c))
        block = jnp.concatenate(
            [ret1[c][:, 0].reshape(4 * ROWS, width), ret2[c][...].reshape(12 * ROWS, width)], 0
        )
        part = dot(w_hi[...], block) + dot(w_lo[...], block)
        own[c][...] = part[0:ROWS]
        zsend[c][...] = part[ROWS:].astype(BF).reshape(NZ - 1, ROWS, width)
        for step in range(1, NZ):
            push(zsend[c].at[step - 1], zrecv[c].at[step - 1], ("rz", c), along_z(-step))

    def finish(c):
        arrived(zrecv[c], ("rz", c))
        total = own[c][...] + jnp.sum(zrecv[c][...].astype(F32), 0)
        out[:, pl.ds(out_at[c], CHUNKS_OUT[c])] = total.astype(BF)

    for tick in range(n_out + 3):
        for stage, lag in ((down, 0), (turn_back, 1), (combine, 2), (finish, 3)):
            if 0 <= tick - lag < n_out:
                stage(tick - lag)

    for ref, key in sent:
        whole(ref, key).wait_send()
    assert len(index) <= send_sem.shape[0]


def layer(tokens, expert_ids, gate_scores, w_gate, w_up, w_down):
    vmem = pltpu.VMEM
    ins = lambda *lead: [vmem((*lead, ROWS, w), BF) for w in CHUNKS_IN]
    outs = lambda *lead: [vmem((*lead, ROWS, w), BF) for w in CHUNKS_OUT]
    sems = 1 + 1 + 1 + 6 * len(CHUNKS_IN) + 3 * len(CHUNKS_OUT)
    scratch = (
        ins(NZ) + ins(3, 4) + ins(4, 4) + ins(3, 4) + ins(4, 4)
        + outs(3, 4) + outs(4, 4) + outs(3, 4) + outs(NZ - 1) + outs(NZ - 1)
        + [vmem((ROWS, w), F32) for w in CHUNKS_OUT]
        + [
            vmem((TOP, ROWS), jnp.int32),
            vmem((TOP, ROWS), F32),
            vmem((NZ, 2 * ROWS, 128), F32),
            vmem((SLOTS, COLUMN), BF),
            vmem((COLUMN, SLOTS), BF),
            vmem((COLUMN, SLOTS), BF),
            vmem((4, 4, ROWS, HID), BF),
            vmem((4, 4, ROWS, HID), BF),
            vmem((SLOTS, HID), F32),
            vmem((SLOTS, HID), F32),
            vmem((2, HALF, HID), BF),
            vmem((2, HALF, HID), BF),
            vmem((HID, HALF), BF),
            vmem((HID, HALF), BF),
            pltpu.SemaphoreType.DMA((7 + len(CHUNKS_IN),)),
            pltpu.SemaphoreType.DMA((sems,)),
            pltpu.SemaphoreType.DMA((sems,)),
        ]
    )
    return pl.pallas_call(
        kernel,
        out_shape=jax.ShapeDtypeStruct((ROWS, HALF), BF),
        in_specs=[pl.BlockSpec(memory_space=pl.ANY)] * 6,
        out_specs=pl.BlockSpec(memory_space=pltpu.VMEM),
        scratch_shapes=scratch,
        compiler_params=pltpu.CompilerParams(
            collective_id=0, has_side_effects=True, vmem_limit_bytes=56 << 20
        ),
    )(tokens, expert_ids.T, gate_scores.T, w_gate, w_up, w_down)


def solution(mesh):
    in_specs = (
        P("expert", None),
        P("expert", None),
        P("expert", None),
        P("expert", None, "rep"),
        P("expert", None, "rep"),
        P("expert", "rep", None),
    )
    return jax.shard_map(layer, mesh=mesh, in_specs=in_specs, out_specs=P("expert", "rep"), check_vma=False)
```

```python
import jax
import jax.numpy as jnp
from jax import lax
from jax.experimental import pallas as pl
from jax.experimental.pallas import tpu as pltpu
from jax.sharding import PartitionSpec as P

NX, NY, NZ = 4, 4, 8
ROWS = 16
TOP = 8
CAP = 2
HALF = 1792
HID = 512
SLOTS = NX * NY * NZ * CAP
COLUMN = NZ * ROWS
PLANE = NX * NY
Z_ORDER = (4, 3, 5, 2, 6, 1, 7)
PLANE_ORDER = (10, 9, 11, 6, 14, 5, 7, 13, 15, 8, 2, 4, 12, 1, 3)
LAG = 2
CHUNKS_IN = (256, 512, 512, 512)
CHUNKS_OUT = (512, 512, 512, 256)
BF = jnp.bfloat16
F32 = jnp.float32


def starts(widths):
    return [sum(widths[:i]) for i in range(len(widths))]


def dot(lhs, rhs):
    return jnp.dot(lhs, rhs, preferred_element_type=F32)


def kernel(tok, ids, sc, wg, wu, wd, out, *scratch):
    names = iter(scratch)
    n_in, n_out = len(CHUNKS_IN), len(CHUNKS_OUT)
    take = lambda n: [next(names) for _ in range(n)]
    zbuf, send, recv, sib = (take(n_in) for _ in range(4))
    outb, ret, zsend, zrecv, own = (take(n_out) for _ in range(5))
    ids_v, sc_v, meta, sel_t, w_hi, w_lo, hid, hid_sib, acc_g, acc_u = take(10)
    wg_v, wu_v, wd_own, wd_sib = take(4)
    local, send_sem, recv_sem = take(3)

    r = lax.axis_index("rep")
    e = lax.axis_index("expert")
    y, z, x = e // 32, (e // 4) % 8, e % 4

    def in_plane(block, sign):
        y_at = (y + sign * (block // 4) + 4) % 4
        x_at = (x + sign * (block % 4) + 4) % 4
        return {"rep": r, "expert": (y_at * 8 + z) * 4 + x_at}

    def along_z(step):
        return {"rep": r, "expert": (y * 8 + (z + step + 8) % 8) * 4 + x}

    sibling = {"rep": 1 - r, "expert": e}

    index = {}

    def sem_of(key):
        return index.setdefault(key, len(index))

    def push(src, dst, key, target):
        at = sem_of(key)
        pltpu.make_async_remote_copy(
            src_ref=src,
            dst_ref=dst,
            send_sem=send_sem.at[at],
            recv_sem=recv_sem.at[at],
            device_id=target,
        ).start()

    def whole(ref, key):
        at = sem_of(key)
        return pltpu.make_async_remote_copy(
            src_ref=ref,
            dst_ref=ref,
            send_sem=send_sem.at[at],
            recv_sem=recv_sem.at[at],
            device_id=sibling,
        )

    sent = []

    def arrived(ref, key):
        whole(ref, key).wait_recv()
        sent.append((ref, key))

    in_at, out_at = starts(CHUNKS_IN), starts(CHUNKS_OUT)
    mine, other = r * HALF, (1 - r) * HALF

    loads = {}

    def load(name, src, dst):
        loads[name] = pltpu.make_async_copy(src, dst, local.at[len(loads)])
        loads[name].start()

    load("ids", ids, ids_v)
    load("sc", sc, sc_v)
    for c, width in enumerate(CHUNKS_IN):
        load(("tok", c), tok.at[:, pl.ds(pl.multiple_of(mine + in_at[c], 128), width)], zbuf[c].at[0])

    barrier = pltpu.get_barrier_semaphore()
    for step in range(1, NZ):
        pl.semaphore_signal(barrier, inc=1, device_id=along_z(step))
    for block in range(1, PLANE):
        pl.semaphore_signal(barrier, inc=1, device_id=in_plane(block, 1))
    pl.semaphore_signal(barrier, inc=1, device_id=sibling)

    for half, base in ((0, mine), (1, other)):
        rows = pl.ds(pl.multiple_of(base, 128), HALF)
        load(("wg", half), wg.at[0, rows, :], wg_v.at[half])
        load(("wu", half), wu.at[0, rows, :], wu_v.at[half])
    load("wd", wd.at[0, :, pl.ds(pl.multiple_of(mine, 128), HALF)], wd_own)
    loads["ids"].wait()
    loads["sc"].wait()
    meta[0, :, 0 : 2 * ROWS] = jnp.concatenate([ids_v[...].astype(F32), sc_v[...]], 1)
    for c in range(n_in):
        loads["tok", c].wait()
    pl.semaphore_wait(barrier, NZ - 1 + PLANE - 1 + 1)

    for step in Z_ORDER:
        push(meta.at[0], meta.at[step], "meta", along_z(step))
    for c in range(n_in):
        for step in Z_ORDER:
            push(zbuf[c].at[0], zbuf[c].at[step], ("z", c), along_z(step))
    push(wd.at[0, :, pl.ds(pl.multiple_of(other, 128), HALF)], wd_sib, "wd", sibling)

    lane = lax.broadcasted_iota(jnp.int32, (ROWS, SLOTS), 1)
    y_to = (y + (lane >> 6)) & 3
    x_to = (x + ((lane >> 4) & 3)) & 3
    named = ((y_to * 8 + z) * 4 + x_to).astype(F32)
    to_row = lax.broadcasted_iota(jnp.int32, (COLUMN, COLUMN), 0)
    from_row = lax.broadcasted_iota(jnp.int32, (COLUMN, COLUMN), 1)
    before = jnp.where(((to_row >> 4) == (from_row >> 4)) & (from_row < to_row), 1.0, 0.0).astype(BF)
    lane_all = lax.broadcasted_iota(jnp.int32, (COLUMN, SLOTS), 1)
    arrived(meta.at[pl.ds(1, NZ - 1)], "meta")
    table = meta[...].reshape(NZ * TOP, 128).T
    members, weights = [], []
    for step in range(NZ):
        expert = jnp.where(((lane >> 1) & 7) == step, named, -1.0)
        member = jnp.zeros((ROWS, SLOTS), F32)
        weight = jnp.zeros((ROWS, SLOTS), F32)
        for k in range(TOP):
            at = step * TOP + k
            hit = table[0:ROWS, at : at + 1] == expert
            member = jnp.where(hit, 1.0, member)
            weight = jnp.where(hit, table[ROWS : 2 * ROWS, at : at + 1], weight)
        members.append(member)
        weights.append(weight)
    member = jnp.concatenate(members, 0)
    weight = jnp.concatenate(weights, 0)
    chosen = dot(before, member.astype(BF)) == (lane_all & 1).astype(F32)
    sel_t[...] = jnp.where(chosen, member, 0.0).T.astype(BF)
    weight = jnp.where(chosen, weight, 0.0)
    high = weight.astype(BF)
    w_hi[...] = high
    w_lo[...] = (weight - high.astype(F32)).astype(BF)

    def select(c):
        width = CHUNKS_IN[c]
        arrived(zbuf[c].at[pl.ds(1, NZ - 1)], ("z", c))
        slots = dot(sel_t[...], zbuf[c][...].reshape(COLUMN, width)).astype(BF)
        slots = slots.reshape(PLANE, ROWS, width)
        recv[c][0] = slots[0]
        send[c][...] = slots[1:]
        for block in PLANE_ORDER:
            push(send[c].at[block - 1], recv[c].at[block], ("p", c), in_plane(block, 1))

    def accumulate(block, half, c, first):
        rows = pl.ds(in_at[c], CHUNKS_IN[c])
        gate = dot(block, wg_v[half, rows, :])
        up = dot(block, wu_v[half, rows, :])
        if first:
            acc_g[...] = gate
            acc_u[...] = up
        else:
            acc_g[...] += gate
            acc_u[...] += up

    def landed(c):
        arrived(recv[c].at[pl.ds(1, PLANE - 1)], ("p", c))
        push(recv[c], sib[c], ("s", c), sibling)
        if c == 0:
            loads["wg", 0].wait()
            loads["wu", 0].wait()
        accumulate(recv[c][...].reshape(SLOTS, CHUNKS_IN[c]), 0, c, c == 0)

    def siblings(c):
        arrived(sib[c], ("s", c))
        if c == 0:
            loads["wg", 1].wait()
            loads["wu", 1].wait()
        accumulate(sib[c][...].reshape(SLOTS, CHUNKS_IN[c]), 1, c, False)

    for tick in range(n_in + 2):
        for stage, lag in ((select, 0), (landed, 1), (siblings, 2)):
            if 0 <= tick - lag < n_in:
                stage(tick - lag)

    gate = acc_g[...]
    hid[...] = (gate / (1.0 + jnp.exp(-gate)) * acc_u[...]).astype(BF)
    push(hid, hid_sib, "hid", sibling)
    loads["wd"].wait()
    arrived(wd_sib, "wd")

    def down(c):
        width = CHUNKS_OUT[c]
        columns = pl.ds(out_at[c], width)
        total = dot(hid[...], wd_own[:, columns])
        if c == 0:
            arrived(hid_sib, "hid")
        total = total + dot(hid_sib[...], wd_sib[:, columns])
        blocks = total.astype(BF).reshape(PLANE, ROWS, width)
        ret[c][0] = blocks[0]
        outb[c][...] = blocks[1:]
        for block in PLANE_ORDER:
            push(outb[c].at[block - 1], ret[c].at[block], ("rp", c), in_plane(block, -1))

    def combine(c):
        width = CHUNKS_OUT[c]
        arrived(ret[c].at[pl.ds(1, PLANE - 1)], ("rp", c))
        block = ret[c][...].reshape(SLOTS, width)
        part = dot(w_hi[...], block) + dot(w_lo[...], block)
        own[c][...] = part[0:ROWS]
        zsend[c][...] = part[ROWS:].astype(BF).reshape(NZ - 1, ROWS, width)
        for step in Z_ORDER:
            push(zsend[c].at[step - 1], zrecv[c].at[step - 1], ("rz", c), along_z(-step))

    def finish(c):
        arrived(zrecv[c], ("rz", c))
        total = own[c][...] + jnp.sum(zrecv[c][...].astype(F32), 0)
        out[:, pl.ds(out_at[c], CHUNKS_OUT[c])] = total.astype(BF)

    for tick in range(n_out + LAG + 1):
        for stage, lag in ((down, 0), (combine, LAG), (finish, LAG + 1)):
            if 0 <= tick - lag < n_out:
                stage(tick - lag)

    for ref, key in sent:
        whole(ref, key).wait_send()
    assert len(index) <= send_sem.shape[0]


def layer(tokens, expert_ids, gate_scores, w_gate, w_up, w_down):
    vmem = pltpu.VMEM
    ins = lambda *lead: [vmem((*lead, ROWS, w), BF) for w in CHUNKS_IN]
    outs = lambda *lead: [vmem((*lead, ROWS, w), BF) for w in CHUNKS_OUT]
    sems = 3 + 3 * len(CHUNKS_IN) + 2 * len(CHUNKS_OUT)
    scratch = (
        ins(NZ) + ins(PLANE - 1) + ins(PLANE) + ins(PLANE)
        + outs(PLANE - 1) + outs(PLANE) + outs(NZ - 1) + outs(NZ - 1)
        + [vmem((ROWS, w), F32) for w in CHUNKS_OUT]
        + [
            vmem((TOP, ROWS), jnp.int32),
            vmem((TOP, ROWS), F32),
            vmem((NZ, TOP, 128), F32),
            vmem((SLOTS, COLUMN), BF),
            vmem((COLUMN, SLOTS), BF),
            vmem((COLUMN, SLOTS), BF),
            vmem((SLOTS, HID), BF),
            vmem((SLOTS, HID), BF),
            vmem((SLOTS, HID), F32),
            vmem((SLOTS, HID), F32),
            vmem((2, HALF, HID), BF),
            vmem((2, HALF, HID), BF),
            vmem((HID, HALF), BF),
            vmem((HID, HALF), BF),
            pltpu.SemaphoreType.DMA((7 + len(CHUNKS_IN),)),
            pltpu.SemaphoreType.DMA((sems,)),
            pltpu.SemaphoreType.DMA((sems,)),
        ]
    )
    return pl.pallas_call(
        kernel,
        out_shape=jax.ShapeDtypeStruct((ROWS, HALF), BF),
        in_specs=[pl.BlockSpec(memory_space=pl.ANY)] * 6,
        out_specs=pl.BlockSpec(memory_space=pltpu.VMEM),
        scratch_shapes=scratch,
        compiler_params=pltpu.CompilerParams(
            collective_id=0, has_side_effects=True, vmem_limit_bytes=56 << 20
        ),
    )(tokens, expert_ids.T, gate_scores.T, w_gate, w_up, w_down)


def solution(mesh):
    in_specs = (
        P("expert", None),
        P("expert", None),
        P("expert", None),
        P("expert", None, "rep"),
        P("expert", None, "rep"),
        P("expert", "rep", None),
    )
    return jax.shard_map(layer, mesh=mesh, in_specs=in_specs, out_specs=P("expert", "rep"), check_vma=False)
```

```python
import jax
import jax.numpy as jnp
from jax import lax
from jax.experimental import pallas as pl
from jax.experimental.pallas import tpu as pltpu
from jax.sharding import PartitionSpec as P

NX, NY, NZ = 4, 4, 8
ROWS = 16
TOP = 8
CAP = 2
HALF = 1792
HID = 512
SLOTS = NX * NY * NZ * CAP
COLUMN = NZ * ROWS
PLANE = NX * NY
Z_ORDER = (4, 3, 5, 2, 6, 1, 7)
PLANE_ORDER = (10, 9, 11, 6, 14, 5, 7, 13, 15, 8, 2, 4, 12, 1, 3)
IN_STEPS = "S0S1S2F0M0S3F1M1X0F2M2X1F3M3X2X3"
OUT_STEPS = "D0D1D2C0D3C1C2N0C3N1N2N3"
CHUNKS_IN = (512, 512, 512, 256)
CHUNKS_OUT = (512, 512, 512, 256)
BF = jnp.bfloat16
F32 = jnp.float32


def starts(widths):
    return [sum(widths[:i]) for i in range(len(widths))]


def dot(lhs, rhs):
    return jnp.dot(lhs, rhs, preferred_element_type=F32)


def kernel(tok, ids, sc, wg, wu, wd, out, *scratch):
    names = iter(scratch)
    n_in, n_out = len(CHUNKS_IN), len(CHUNKS_OUT)
    take = lambda n: [next(names) for _ in range(n)]
    zbuf, send, recv, sib = (take(n_in) for _ in range(4))
    outb, ret, zsend, zrecv, own = (take(n_out) for _ in range(5))
    ids_v, sc_v, meta, sel_t, w_hi, w_lo, hid, hid_sib, acc_g, acc_u = take(10)
    wg_v, wu_v, wd_own, wd_sib = take(4)
    local, send_sem, recv_sem = take(3)

    r = lax.axis_index("rep")
    e = lax.axis_index("expert")
    y, z, x = e // 32, (e // 4) % 8, e % 4

    def in_plane(block, sign):
        y_at = (y + sign * (block // 4) + 4) % 4
        x_at = (x + sign * (block % 4) + 4) % 4
        return {"rep": r, "expert": (y_at * 8 + z) * 4 + x_at}

    def along_z(step):
        return {"rep": r, "expert": (y * 8 + (z + step + 8) % 8) * 4 + x}

    sibling = {"rep": 1 - r, "expert": e}

    index = {}

    def sem_of(key):
        return index.setdefault(key, len(index))

    def push(src, dst, key, target):
        at = sem_of(key)
        pltpu.make_async_remote_copy(
            src_ref=src,
            dst_ref=dst,
            send_sem=send_sem.at[at],
            recv_sem=recv_sem.at[at],
            device_id=target,
        ).start()

    def whole(ref, key):
        at = sem_of(key)
        return pltpu.make_async_remote_copy(
            src_ref=ref,
            dst_ref=ref,
            send_sem=send_sem.at[at],
            recv_sem=recv_sem.at[at],
            device_id=sibling,
        )

    sent = []

    def arrived(ref, key):
        whole(ref, key).wait_recv()
        sent.append((ref, key))

    in_at, out_at = starts(CHUNKS_IN), starts(CHUNKS_OUT)
    mine, other = r * HALF, (1 - r) * HALF

    loads = {}

    def load(name, src, dst):
        loads[name] = pltpu.make_async_copy(src, dst, local.at[len(loads)])
        loads[name].start()

    load("ids", ids, ids_v)
    load("sc", sc, sc_v)
    for c, width in enumerate(CHUNKS_IN):
        load(("tok", c), tok.at[:, pl.ds(pl.multiple_of(mine + in_at[c], 128), width)], zbuf[c].at[0])

    barrier = pltpu.get_barrier_semaphore()
    for step in range(1, NZ):
        pl.semaphore_signal(barrier, inc=1, device_id=along_z(step))
    for block in range(1, PLANE):
        pl.semaphore_signal(barrier, inc=1, device_id=in_plane(block, 1))
    pl.semaphore_signal(barrier, inc=1, device_id=sibling)

    loads["ids"].wait()
    loads["sc"].wait()
    high = sc_v[...].astype(BF).astype(F32)
    meta[0, :, 0 : 3 * ROWS] = jnp.concatenate([ids_v[...].astype(F32), high, sc_v[...] - high], 1).astype(BF)
    for c in range(n_in):
        loads["tok", c].wait()
    pl.semaphore_wait(barrier, NZ - 1 + PLANE - 1 + 1)

    for step in Z_ORDER:
        push(meta.at[0], meta.at[step], "meta", along_z(step))
    for c in range(n_in):
        for step in Z_ORDER:
            push(zbuf[c].at[0], zbuf[c].at[step], ("z", c), along_z(step))

    lane = lax.broadcasted_iota(jnp.int32, (ROWS, SLOTS), 1)
    y_to = (y + (lane >> 6)) & 3
    x_to = (x + ((lane >> 4) & 3)) & 3
    named = ((y_to * 8 + z) * 4 + x_to).astype(F32)
    to_row = lax.broadcasted_iota(jnp.int32, (COLUMN, COLUMN), 0)
    from_row = lax.broadcasted_iota(jnp.int32, (COLUMN, COLUMN), 1)
    before = jnp.where(((to_row >> 4) == (from_row >> 4)) & (from_row < to_row), 1.0, 0.0).astype(BF)
    lane_all = lax.broadcasted_iota(jnp.int32, (COLUMN, SLOTS), 1)
    arrived(meta.at[pl.ds(1, NZ - 1)], "meta")
    for half, base in ((0, mine), (1, other)):
        rows = pl.ds(pl.multiple_of(base, 128), HALF)
        load(("wg", half), wg.at[0, rows, :], wg_v.at[half])
        load(("wu", half), wu.at[0, rows, :], wu_v.at[half])
    load("wd", wd.at[0, :, pl.ds(pl.multiple_of(mine, 128), HALF)], wd_own)
    push(wd.at[0, :, pl.ds(pl.multiple_of(other, 128), HALF)], wd_sib, "wd", sibling)
    table = meta[...].reshape(NZ * TOP, 128).astype(F32).T
    members, highs, lows = [], [], []
    for step in range(NZ):
        expert = jnp.where(((lane >> 1) & 7) == step, named, -1.0)
        member = jnp.zeros((ROWS, SLOTS), F32)
        high = jnp.zeros((ROWS, SLOTS), F32)
        low = jnp.zeros((ROWS, SLOTS), F32)
        for k in range(TOP):
            at = step * TOP + k
            hit = table[0:ROWS, at : at + 1] == expert
            member = jnp.where(hit, 1.0, member)
            high = jnp.where(hit, table[ROWS : 2 * ROWS, at : at + 1], high)
            low = jnp.where(hit, table[2 * ROWS : 3 * ROWS, at : at + 1], low)
        members.append(member)
        highs.append(high)
        lows.append(low)
    member = jnp.concatenate(members, 0)
    chosen = dot(before, member.astype(BF)) == (lane_all & 1).astype(F32)
    sel_t[...] = jnp.where(chosen, member, 0.0).T.astype(BF)
    w_hi[...] = jnp.where(chosen, jnp.concatenate(highs, 0), 0.0).astype(BF)
    w_lo[...] = jnp.where(chosen, jnp.concatenate(lows, 0), 0.0).astype(BF)

    def select(c):
        width = CHUNKS_IN[c]
        arrived(zbuf[c].at[pl.ds(1, NZ - 1)], ("z", c))
        slots = dot(sel_t[...], zbuf[c][...].reshape(COLUMN, width)).astype(BF)
        slots = slots.reshape(PLANE, ROWS, width)
        recv[c][0] = slots[0]
        send[c][...] = slots[1:]
        for block in PLANE_ORDER:
            push(send[c].at[block - 1], recv[c].at[block], ("p", c), in_plane(block, 1))

    def accumulate(block, half, c, first):
        rows = pl.ds(in_at[c], CHUNKS_IN[c])
        gate = dot(block, wg_v[half, rows, :])
        up = dot(block, wu_v[half, rows, :])
        if first:
            acc_g[...] = gate
            acc_u[...] = up
        else:
            acc_g[...] += gate
            acc_u[...] += up

    def landed(c):
        arrived(recv[c].at[pl.ds(1, PLANE - 1)], ("p", c))
        push(recv[c], sib[c], ("s", c), sibling)

    def halves(c):
        if c == 0:
            loads["wg", 0].wait()
            loads["wu", 0].wait()
        accumulate(recv[c][...].reshape(SLOTS, CHUNKS_IN[c]), 0, c, c == 0)

    def siblings(c):
        arrived(sib[c], ("s", c))
        if c == 0:
            loads["wg", 1].wait()
            loads["wu", 1].wait()
        accumulate(sib[c][...].reshape(SLOTS, CHUNKS_IN[c]), 1, c, False)

    stages = {"S": select, "F": landed, "M": halves, "X": siblings}
    for name, c in zip(IN_STEPS[::2], IN_STEPS[1::2]):
        stages[name](int(c))

    gate = acc_g[...]
    hid[...] = (gate / (1.0 + jnp.exp(-gate)) * acc_u[...]).astype(BF)
    push(hid, hid_sib, "hid", sibling)
    loads["wd"].wait()
    arrived(wd_sib, "wd")

    def down(c):
        width = CHUNKS_OUT[c]
        columns = pl.ds(out_at[c], width)
        total = dot(hid[...], wd_own[:, columns])
        if c == 0:
            arrived(hid_sib, "hid")
        total = total + dot(hid_sib[...], wd_sib[:, columns])
        blocks = total.astype(BF).reshape(PLANE, ROWS, width)
        ret[c][0] = blocks[0]
        outb[c][...] = blocks[1:]
        for block in PLANE_ORDER:
            push(outb[c].at[block - 1], ret[c].at[block], ("rp", c), in_plane(block, -1))

    def combine(c):
        width = CHUNKS_OUT[c]
        arrived(ret[c].at[pl.ds(1, PLANE - 1)], ("rp", c))
        block = ret[c][...].reshape(SLOTS, width)
        part = dot(w_hi[...], block) + dot(w_lo[...], block)
        own[c][...] = part[0:ROWS]
        zsend[c][...] = part[ROWS:].astype(BF).reshape(NZ - 1, ROWS, width)
        for step in Z_ORDER:
            push(zsend[c].at[step - 1], zrecv[c].at[step - 1], ("rz", c), along_z(-step))

    def finish(c):
        arrived(zrecv[c], ("rz", c))
        total = own[c][...] + jnp.sum(zrecv[c][...].astype(F32), 0)
        out[:, pl.ds(out_at[c], CHUNKS_OUT[c])] = total.astype(BF)

    stages = {"D": down, "C": combine, "N": finish}
    for name, c in zip(OUT_STEPS[::2], OUT_STEPS[1::2]):
        stages[name](int(c))

    for ref, key in sent:
        whole(ref, key).wait_send()
    assert len(index) <= send_sem.shape[0]


def layer(tokens, expert_ids, gate_scores, w_gate, w_up, w_down):
    vmem = pltpu.VMEM
    ins = lambda *lead: [vmem((*lead, ROWS, w), BF) for w in CHUNKS_IN]
    outs = lambda *lead: [vmem((*lead, ROWS, w), BF) for w in CHUNKS_OUT]
    sems = 3 + 3 * len(CHUNKS_IN) + 2 * len(CHUNKS_OUT)
    scratch = (
        ins(NZ) + ins(PLANE - 1) + ins(PLANE) + ins(PLANE)
        + outs(PLANE - 1) + outs(PLANE) + outs(NZ - 1) + outs(NZ - 1)
        + [vmem((ROWS, w), F32) for w in CHUNKS_OUT]
        + [
            vmem((TOP, ROWS), jnp.int32),
            vmem((TOP, ROWS), F32),
            vmem((NZ, TOP, 128), BF),
            vmem((SLOTS, COLUMN), BF),
            vmem((COLUMN, SLOTS), BF),
            vmem((COLUMN, SLOTS), BF),
            vmem((SLOTS, HID), BF),
            vmem((SLOTS, HID), BF),
            vmem((SLOTS, HID), F32),
            vmem((SLOTS, HID), F32),
            vmem((2, HALF, HID), BF),
            vmem((2, HALF, HID), BF),
            vmem((HID, HALF), BF),
            vmem((HID, HALF), BF),
            pltpu.SemaphoreType.DMA((7 + len(CHUNKS_IN),)),
            pltpu.SemaphoreType.DMA((sems,)),
            pltpu.SemaphoreType.DMA((sems,)),
        ]
    )
    return pl.pallas_call(
        kernel,
        out_shape=jax.ShapeDtypeStruct((ROWS, HALF), BF),
        in_specs=[pl.BlockSpec(memory_space=pl.ANY)] * 6,
        out_specs=pl.BlockSpec(memory_space=pltpu.VMEM),
        scratch_shapes=scratch,
        compiler_params=pltpu.CompilerParams(
            collective_id=0, has_side_effects=True, vmem_limit_bytes=56 << 20
        ),
    )(tokens, expert_ids.T, gate_scores.T, w_gate, w_up, w_down)


def solution(mesh):
    in_specs = (
        P("expert", None),
        P("expert", None),
        P("expert", None),
        P("expert", None, "rep"),
        P("expert", None, "rep"),
        P("expert", "rep", None),
    )
    return jax.shard_map(layer, mesh=mesh, in_specs=in_specs, out_specs=P("expert", "rep"), check_vma=False)
```

```python
import jax
import jax.numpy as jnp
from jax import lax
from jax.experimental import pallas as pl
from jax.experimental.pallas import tpu as pltpu
from jax.sharding import PartitionSpec as P

NX, NY, NZ = 4, 4, 8
ROWS = 16
TOP = 8
CAP = 2
HALF = 1792
HID = 512
SLOTS = NX * NY * NZ * CAP
PLANE = NX * NY
Z_ORDER = (4, 2, 6, 3, 5, 1, 7)
PLANE_ORDER = (10, 9, 11, 6, 14, 5, 7, 13, 15, 8, 2, 4, 12, 1, 3)
STEPS = "S00 S01 S10 F00 M00 S11 F01 M01 X00 X01 H00 F10 M10 D00 D01 F11 M11 X10 X11 H10 D10 D11 C00 C01 C10 C11 N00 N01 N10 N11"
CHUNKS_IN = ((768, 1024), (1024, 768))
CHUNKS_OUT = ((1024, 768), (1024, 768))
GROUPS = ((0, 2, 4, 6), (1, 3, 5, 7))
Z_ORDERS = ((2, 1, 3), (1, 2, 0, 3))
PER = len(GROUPS[0])
GROUP_ROWS = PER * ROWS
BLOCK = PER * CAP
GROUP_SLOTS = SLOTS // 2
BF = jnp.bfloat16
F32 = jnp.float32


def starts(widths):
    return [sum(widths[:i]) for i in range(len(widths))]


def dot(lhs, rhs):
    return jnp.dot(lhs, rhs, preferred_element_type=F32)


def kernel(tok, ids, sc, wg, wu, wd, out, *scratch):
    names = iter(scratch)
    take = lambda n: [next(names) for _ in range(n)]
    per_group = lambda lists: [take(len(widths)) for widths in lists]
    zbuf, send, recv, sib = (per_group(CHUNKS_IN) for _ in range(4))
    outb, ret, zsend, zrecv = (per_group(CHUNKS_OUT) for _ in range(4))
    ids_v, sc_v, meta, sel_t, w_hi, w_lo, hid, hid_sib, acc_g, acc_u, own = take(11)
    wg_v, wu_v, wd_own, wd_sib, tok_v = take(5)
    local, send_sem, recv_sem = take(3)

    r = lax.axis_index("rep")
    e = lax.axis_index("expert")
    y, z, x = e // 32, (e // 4) % 8, e % 4

    def in_plane(block, sign):
        y_at = (y + sign * (block // 4) + 4) % 4
        x_at = (x + sign * (block % 4) + 4) % 4
        return {"rep": r, "expert": (y_at * 8 + z) * 4 + x_at}

    def along_z(step):
        return {"rep": r, "expert": (y * 8 + (z + step + 8) % 8) * 4 + x}

    sibling = {"rep": 1 - r, "expert": e}

    index = {}

    def sem_of(key):
        return index.setdefault(key, len(index))

    def push(src, dst, key, target):
        at = sem_of(key)
        pltpu.make_async_remote_copy(
            src_ref=src,
            dst_ref=dst,
            send_sem=send_sem.at[at],
            recv_sem=recv_sem.at[at],
            device_id=target,
        ).start()

    def whole(ref, key):
        at = sem_of(key)
        return pltpu.make_async_remote_copy(
            src_ref=ref,
            dst_ref=ref,
            send_sem=send_sem.at[at],
            recv_sem=recv_sem.at[at],
            device_id=sibling,
        )

    sent = []

    def arrived(ref, key):
        whole(ref, key).wait_recv()
        sent.append((ref, key))

    in_at, out_at = [starts(w) for w in CHUNKS_IN], [starts(w) for w in CHUNKS_OUT]
    mine, other = r * HALF, (1 - r) * HALF

    loads = {}

    def load(name, src, dst):
        loads[name] = pltpu.make_async_copy(src, dst, local.at[len(loads)])
        loads[name].start()

    load("ids", ids, ids_v)
    load("sc", sc, sc_v)
    load("tok", tok.at[:, pl.ds(pl.multiple_of(mine, 128), HALF)], tok_v)

    barrier = pltpu.get_barrier_semaphore()
    for step in range(1, NZ):
        pl.semaphore_signal(barrier, inc=1, device_id=along_z(step))
    for block in range(1, PLANE):
        pl.semaphore_signal(barrier, inc=1, device_id=in_plane(block, 1))
    pl.semaphore_signal(barrier, inc=1, device_id=sibling)

    loads["ids"].wait()
    loads["sc"].wait()
    high = sc_v[...].astype(BF).astype(F32)
    meta[0, :, 0 : 3 * ROWS] = jnp.concatenate([ids_v[...].astype(F32), high, sc_v[...] - high], 1).astype(BF)
    loads["tok"].wait()
    for c, width in enumerate(CHUNKS_IN[0]):
        zbuf[0][c][0] = tok_v[:, in_at[0][c] : in_at[0][c] + width]
    pl.semaphore_wait(barrier, NZ - 1 + PLANE - 1 + 1)

    for step in Z_ORDER:
        push(meta.at[0], meta.at[step], "meta", along_z(step))
    for g in range(2):
        for c, width in enumerate(CHUNKS_IN[g]):
            for p in Z_ORDERS[g]:
                push(
                    tok_v.at[:, pl.ds(in_at[g][c], width)],
                    zbuf[g][c].at[p],
                    ("z", g, c),
                    along_z(GROUPS[g][p]),
                )

    lane = lax.broadcasted_iota(jnp.int32, (ROWS, GROUP_SLOTS), 1)
    y_to = (y + (lane >> 5)) & 3
    x_to = (x + ((lane >> 3) & 3)) & 3
    named = ((y_to * 8 + z) * 4 + x_to).astype(F32)
    to_row = lax.broadcasted_iota(jnp.int32, (GROUP_ROWS, GROUP_ROWS), 0)
    from_row = lax.broadcasted_iota(jnp.int32, (GROUP_ROWS, GROUP_ROWS), 1)
    before = jnp.where(((to_row >> 4) == (from_row >> 4)) & (from_row < to_row), 1.0, 0.0).astype(BF)
    lane_all = lax.broadcasted_iota(jnp.int32, (GROUP_ROWS, GROUP_SLOTS), 1)
    arrived(meta.at[pl.ds(1, NZ - 1)], "meta")
    for half, base in ((0, mine), (1, other)):
        rows = pl.ds(pl.multiple_of(base, 128), HALF)
        load(("wg", half), wg.at[0, rows, :], wg_v.at[half])
        load(("wu", half), wu.at[0, rows, :], wu_v.at[half])
    load("wd", wd.at[0, :, pl.ds(pl.multiple_of(mine, 128), HALF)], wd_own)
    push(wd.at[0, :, pl.ds(pl.multiple_of(other, 128), HALF)], wd_sib, "wd", sibling)
    table = meta[...].reshape(NZ * TOP, 128).astype(F32).T
    for g in range(2):
        members, highs, lows = [], [], []
        for p, step in enumerate(GROUPS[g]):
            expert = jnp.where(((lane >> 1) & 3) == p, named, -1.0)
            member = jnp.zeros((ROWS, GROUP_SLOTS), F32)
            high = jnp.zeros((ROWS, GROUP_SLOTS), F32)
            low = jnp.zeros((ROWS, GROUP_SLOTS), F32)
            for k in range(TOP):
                at = step * TOP + k
                hit = table[0:ROWS, at : at + 1] == expert
                member = jnp.where(hit, 1.0, member)
                high = jnp.where(hit, table[ROWS : 2 * ROWS, at : at + 1], high)
                low = jnp.where(hit, table[2 * ROWS : 3 * ROWS, at : at + 1], low)
            members.append(member)
            highs.append(high)
            lows.append(low)
        member = jnp.concatenate(members, 0)
        chosen = dot(before, member.astype(BF)) == (lane_all & 1).astype(F32)
        sel_t[g] = jnp.where(chosen, member, 0.0).T.astype(BF)
        w_hi[g] = jnp.where(chosen, jnp.concatenate(highs, 0), 0.0).astype(BF)
        w_lo[g] = jnp.where(chosen, jnp.concatenate(lows, 0), 0.0).astype(BF)

    ready = set()

    def once(*keys):
        for key in keys:
            if key not in ready:
                ready.add(key)
                loads[key].wait()

    def far(g):
        return pl.ds(1 - g, PER - 1 + g)

    def select(g, c):
        width = CHUNKS_IN[g][c]
        arrived(zbuf[g][c].at[far(g)], ("z", g, c))
        slots = dot(sel_t[g], zbuf[g][c][...].reshape(GROUP_ROWS, width)).astype(BF)
        slots = slots.reshape(PLANE, BLOCK, width)
        recv[g][c][0] = slots[0]
        send[g][c][...] = slots[1:]
        for block in PLANE_ORDER:
            push(send[g][c].at[block - 1], recv[g][c].at[block], ("p", g, c), in_plane(block, 1))

    def accumulate(g, block, half, c, first):
        rows = pl.ds(in_at[g][c], CHUNKS_IN[g][c])
        gate = dot(block, wg_v[half, rows, :])
        up = dot(block, wu_v[half, rows, :])
        if first:
            acc_g[g] = gate
            acc_u[g] = up
        else:
            acc_g[g] += gate
            acc_u[g] += up

    def forward(g, c):
        arrived(recv[g][c].at[pl.ds(1, PLANE - 1)], ("p", g, c))
        push(recv[g][c], sib[g][c], ("s", g, c), sibling)

    def halves(g, c):
        once(("wg", 0), ("wu", 0))
        accumulate(g, recv[g][c][...].reshape(GROUP_SLOTS, CHUNKS_IN[g][c]), 0, c, c == 0)

    def siblings(g, c):
        arrived(sib[g][c], ("s", g, c))
        once(("wg", 1), ("wu", 1))
        accumulate(g, sib[g][c][...].reshape(GROUP_SLOTS, CHUNKS_IN[g][c]), 1, c, False)

    def hidden(g, c):
        gate = acc_g[g]
        hid[g] = (gate / (1.0 + jnp.exp(-gate)) * acc_u[g]).astype(BF)
        push(hid.at[g], hid_sib.at[g], ("hid", g), sibling)

    def down(g, c):
        width = CHUNKS_OUT[g][c]
        columns = pl.ds(out_at[g][c], width)
        once("wd")
        total = dot(hid[g], wd_own[:, columns])
        if c == 0:
            if g == 0:
                arrived(wd_sib, "wd")
            arrived(hid_sib.at[g], ("hid", g))
        total = total + dot(hid_sib[g], wd_sib[:, columns])
        blocks = total.astype(BF).reshape(PLANE, BLOCK, width)
        ret[g][c][0] = blocks[0]
        outb[g][c][...] = blocks[1:]
        for block in PLANE_ORDER:
            push(outb[g][c].at[block - 1], ret[g][c].at[block], ("rp", g, c), in_plane(block, -1))

    def combine(g, c):
        width = CHUNKS_OUT[g][c]
        arrived(ret[g][c].at[pl.ds(1, PLANE - 1)], ("rp", g, c))
        block = ret[g][c][...].reshape(GROUP_SLOTS, width)
        part = dot(w_hi[g], block) + dot(w_lo[g], block)
        if g == 0:
            own[:, pl.ds(out_at[g][c], width)] = part[0:ROWS]
        zsend[g][c][...] = part.astype(BF).reshape(PER, ROWS, width)
        for p in Z_ORDERS[g]:
            push(zsend[g][c].at[p], zrecv[g][c].at[p], ("rz", g, c), along_z(-GROUPS[g][p]))

    def finish(g, c):
        arrived(zrecv[g][c].at[far(g)], ("rz", g, c))
        columns = pl.ds(out_at[g][c], CHUNKS_OUT[g][c])
        total = own[:, columns] + jnp.sum(zrecv[g][c][far(g)].astype(F32), 0)
        if g == 0:
            own[:, columns] = total
        else:
            out[:, columns] = total.astype(BF)

    stages = {
        "S": select, "F": forward, "M": halves, "X": siblings,
        "H": hidden, "D": down, "C": combine, "N": finish,
    }
    for name, g, c in STEPS.split():
        stages[name](int(g), int(c))

    for ref, key in sent:
        whole(ref, key).wait_send()
    assert len(index) <= send_sem.shape[0]


def layer(tokens, expert_ids, gate_scores, w_gate, w_up, w_down):
    vmem = pltpu.VMEM
    ins = lambda *lead: [vmem((*lead, w), BF) for widths in CHUNKS_IN for w in widths]
    outs = lambda *lead: [vmem((*lead, w), BF) for widths in CHUNKS_OUT for w in widths]
    sems = 4 + 3 * len(sum(CHUNKS_IN, ())) + 2 * len(sum(CHUNKS_OUT, ()))
    scratch = (
        ins(PER, ROWS) + ins(PLANE - 1, BLOCK) + ins(PLANE, BLOCK) + ins(PLANE, BLOCK)
        + outs(PLANE - 1, BLOCK) + outs(PLANE, BLOCK) + outs(PER, ROWS) + outs(PER, ROWS)
        + [
            vmem((TOP, ROWS), jnp.int32),
            vmem((TOP, ROWS), F32),
            vmem((NZ, TOP, 128), BF),
            vmem((2, GROUP_SLOTS, GROUP_ROWS), BF),
            vmem((2, GROUP_ROWS, GROUP_SLOTS), BF),
            vmem((2, GROUP_ROWS, GROUP_SLOTS), BF),
            vmem((2, GROUP_SLOTS, HID), BF),
            vmem((2, GROUP_SLOTS, HID), BF),
            vmem((2, GROUP_SLOTS, HID), F32),
            vmem((2, GROUP_SLOTS, HID), F32),
            vmem((ROWS, HALF), F32),
            vmem((2, HALF, HID), BF),
            vmem((2, HALF, HID), BF),
            vmem((HID, HALF), BF),
            vmem((HID, HALF), BF),
            vmem((ROWS, HALF), BF),
            pltpu.SemaphoreType.DMA((8,)),
            pltpu.SemaphoreType.DMA((sems,)),
            pltpu.SemaphoreType.DMA((sems,)),
        ]
    )
    return pl.pallas_call(
        kernel,
        out_shape=jax.ShapeDtypeStruct((ROWS, HALF), BF),
        in_specs=[pl.BlockSpec(memory_space=pl.ANY)] * 6,
        out_specs=pl.BlockSpec(memory_space=pltpu.VMEM),
        scratch_shapes=scratch,
        compiler_params=pltpu.CompilerParams(
            collective_id=0, has_side_effects=True, vmem_limit_bytes=56 << 20
        ),
    )(tokens, expert_ids.T, gate_scores.T, w_gate, w_up, w_down)


def solution(mesh):
    in_specs = (
        P("expert", None),
        P("expert", None),
        P("expert", None),
        P("expert", None, "rep"),
        P("expert", None, "rep"),
        P("expert", "rep", None),
    )
    return jax.shard_map(layer, mesh=mesh, in_specs=in_specs, out_specs=P("expert", "rep"), check_vma=False)
```

```python
import jax
import jax.numpy as jnp
from jax import lax
from jax.experimental import pallas as pl
from jax.experimental.pallas import tpu as pltpu
from jax.sharding import PartitionSpec as P

NX, NY, NZ = 4, 4, 8
ROWS = 16
TOP = 8
CAP = 2
HALF = 1792
HID = 512
SLOTS = NX * NY * NZ * CAP
PLANE = NX * NY
Z_ORDER = (4, 2, 6, 3, 5, 1, 7)
PLANE_ORDER = (10, 9, 11, 6, 14, 5, 7, 13, 15, 8, 2, 4, 12, 1, 3)
STEPS = (
    "T00", "S00", "S01", "T10", "S10", "F00", "M00", "S11", "F01", "M01", "X00", "X01",
    "H00", "F10", "M10", "D00", "D01", "F11", "M11", "X10", "X11", "H10",
    "D10", "D11", "C00", "C01", "C10", "C11", "N00", "N01", "N10", "N11",
)
CHUNKS_IN = ((768, 1024), (1024, 768))
CHUNKS_OUT = ((1024, 768), (1024, 768))
GROUPS = ((0, 2, 4, 6), (1, 3, 5, 7))
Z_ORDERS = ((2, 1, 3), (1, 2, 0, 3))
PER = len(GROUPS[0])
GROUP_ROWS = PER * ROWS
BLOCK = PER * CAP
GROUP_SLOTS = SLOTS // 2
BF = jnp.bfloat16
F32 = jnp.float32


def starts(widths):
    return [sum(widths[:i]) for i in range(len(widths))]


def dot(lhs, rhs):
    return jnp.dot(lhs, rhs, preferred_element_type=F32)


def kernel(tok, ids, sc, wg, wu, wd, out, *scratch):
    names = iter(scratch)
    take = lambda n: [next(names) for _ in range(n)]
    per_group = lambda lists: [take(len(widths)) for widths in lists]
    zbuf, send, recv, sib = (per_group(CHUNKS_IN) for _ in range(4))
    outb, ret, zsend, zrecv = (per_group(CHUNKS_OUT) for _ in range(4))
    ids_v, sc_v, meta, sel_t, w_hi, w_lo, hid, hid_sib, acc_g, acc_u, own = take(11)
    wg_v, wu_v, wd_own, wd_sib, tok_v = take(5)
    local, send_sem, recv_sem = take(3)

    r = lax.axis_index("rep")
    e = lax.axis_index("expert")
    y, z, x = e // 32, (e // 4) % 8, e % 4

    def in_plane(block, sign):
        y_at = (y + sign * (block // 4) + 4) % 4
        x_at = (x + sign * (block % 4) + 4) % 4
        return {"rep": r, "expert": (y_at * 8 + z) * 4 + x_at}

    def along_z(step):
        return {"rep": r, "expert": (y * 8 + (z + step + 8) % 8) * 4 + x}

    sibling = {"rep": 1 - r, "expert": e}

    index = {}

    def sem_of(key):
        return index.setdefault(key, len(index))

    def push(src, dst, key, target):
        at = sem_of(key)
        pltpu.make_async_remote_copy(
            src_ref=src,
            dst_ref=dst,
            send_sem=send_sem.at[at],
            recv_sem=recv_sem.at[at],
            device_id=target,
        ).start()

    def whole(ref, key):
        at = sem_of(key)
        return pltpu.make_async_remote_copy(
            src_ref=ref,
            dst_ref=ref,
            send_sem=send_sem.at[at],
            recv_sem=recv_sem.at[at],
            device_id=sibling,
        )

    sent = []

    def arrived(ref, key):
        whole(ref, key).wait_recv()
        sent.append((ref, key))

    in_at, out_at = [starts(w) for w in CHUNKS_IN], [starts(w) for w in CHUNKS_OUT]
    mine, other = r * HALF, (1 - r) * HALF

    loads = {}

    def load(name, src, dst):
        loads[name] = pltpu.make_async_copy(src, dst, local.at[len(loads)])
        loads[name].start()

    load("ids", ids, ids_v)
    load("sc", sc, sc_v)
    load("tok", tok.at[:, pl.ds(pl.multiple_of(mine, 128), HALF)], tok_v)

    barrier = pltpu.get_barrier_semaphore()
    for step in range(1, NZ):
        pl.semaphore_signal(barrier, inc=1, device_id=along_z(step))
    for block in range(1, PLANE):
        pl.semaphore_signal(barrier, inc=1, device_id=in_plane(block, 1))
    pl.semaphore_signal(barrier, inc=1, device_id=sibling)

    loads["ids"].wait()
    loads["sc"].wait()
    high = sc_v[...].astype(BF).astype(F32)
    meta[0, :, 0 : 3 * ROWS] = jnp.concatenate([ids_v[...].astype(F32), high, sc_v[...] - high], 1).astype(BF)
    loads["tok"].wait()
    for c, width in enumerate(CHUNKS_IN[0]):
        zbuf[0][c][0] = tok_v[:, in_at[0][c] : in_at[0][c] + width]
    pl.semaphore_wait(barrier, NZ - 1 + PLANE - 1 + 1)

    for step in Z_ORDER:
        push(meta.at[0], meta.at[step], "meta", along_z(step))
    for g in range(2):
        for c, width in enumerate(CHUNKS_IN[g]):
            for p in Z_ORDERS[g]:
                push(
                    tok_v.at[:, pl.ds(in_at[g][c], width)],
                    zbuf[g][c].at[p],
                    ("z", g, c),
                    along_z(GROUPS[g][p]),
                )

    lane = lax.broadcasted_iota(jnp.int32, (ROWS, GROUP_SLOTS), 1)
    y_to = (y + (lane >> 5)) & 3
    x_to = (x + ((lane >> 3) & 3)) & 3
    named = ((y_to * 8 + z) * 4 + x_to).astype(F32)
    to_row = lax.broadcasted_iota(jnp.int32, (GROUP_ROWS, GROUP_ROWS), 0)
    from_row = lax.broadcasted_iota(jnp.int32, (GROUP_ROWS, GROUP_ROWS), 1)
    before = jnp.where(((to_row >> 4) == (from_row >> 4)) & (from_row < to_row), 1.0, 0.0).astype(BF)
    lane_all = lax.broadcasted_iota(jnp.int32, (GROUP_ROWS, GROUP_SLOTS), 1)
    arrived(meta.at[pl.ds(1, NZ - 1)], "meta")
    for half, base in ((0, mine), (1, other)):
        rows = pl.ds(pl.multiple_of(base, 128), HALF)
        load(("wg", half), wg.at[0, rows, :], wg_v.at[half])
        load(("wu", half), wu.at[0, rows, :], wu_v.at[half])
    load("wd", wd.at[0, :, pl.ds(pl.multiple_of(mine, 128), HALF)], wd_own)
    push(wd.at[0, :, pl.ds(pl.multiple_of(other, 128), HALF)], wd_sib, "wd", sibling)
    table = meta[...].reshape(NZ * TOP, 128).astype(F32).T
    def tables(g, c):
        members, highs, lows = [], [], []
        for p, step in enumerate(GROUPS[g]):
            expert = jnp.where(((lane >> 1) & 3) == p, named, -1.0)
            member = jnp.zeros((ROWS, GROUP_SLOTS), F32)
            high = jnp.zeros((ROWS, GROUP_SLOTS), F32)
            low = jnp.zeros((ROWS, GROUP_SLOTS), F32)
            for k in range(TOP):
                at = step * TOP + k
                hit = table[0:ROWS, at : at + 1] == expert
                member = jnp.where(hit, 1.0, member)
                high = jnp.where(hit, table[ROWS : 2 * ROWS, at : at + 1], high)
                low = jnp.where(hit, table[2 * ROWS : 3 * ROWS, at : at + 1], low)
            members.append(member)
            highs.append(high)
            lows.append(low)
        member = jnp.concatenate(members, 0)
        chosen = dot(before, member.astype(BF)) == (lane_all & 1).astype(F32)
        sel_t[g] = jnp.where(chosen, member, 0.0).T.astype(BF)
        w_hi[g] = jnp.where(chosen, jnp.concatenate(highs, 0), 0.0).astype(BF)
        w_lo[g] = jnp.where(chosen, jnp.concatenate(lows, 0), 0.0).astype(BF)

    ready = set()

    def once(*keys):
        for key in keys:
            if key not in ready:
                ready.add(key)
                loads[key].wait()

    def far(g):
        return pl.ds(1 - g, PER - 1 + g)

    def select(g, c):
        width = CHUNKS_IN[g][c]
        arrived(zbuf[g][c].at[far(g)], ("z", g, c))
        slots = dot(sel_t[g], zbuf[g][c][...].reshape(GROUP_ROWS, width)).astype(BF)
        slots = slots.reshape(PLANE, BLOCK, width)
        recv[g][c][0] = slots[0]
        send[g][c][...] = slots[1:]
        for block in PLANE_ORDER:
            push(send[g][c].at[block - 1], recv[g][c].at[block], ("p", g, c), in_plane(block, 1))

    def accumulate(g, block, half, c, first):
        rows = pl.ds(in_at[g][c], CHUNKS_IN[g][c])
        gate = dot(block, wg_v[half, rows, :])
        up = dot(block, wu_v[half, rows, :])
        if first:
            acc_g[g] = gate
            acc_u[g] = up
        else:
            acc_g[g] += gate
            acc_u[g] += up

    def forward(g, c):
        arrived(recv[g][c].at[pl.ds(1, PLANE - 1)], ("p", g, c))
        push(recv[g][c], sib[g][c], ("s", g, c), sibling)

    def halves(g, c):
        once(("wg", 0), ("wu", 0))
        accumulate(g, recv[g][c][...].reshape(GROUP_SLOTS, CHUNKS_IN[g][c]), 0, c, c == 0)

    def siblings(g, c):
        arrived(sib[g][c], ("s", g, c))
        once(("wg", 1), ("wu", 1))
        accumulate(g, sib[g][c][...].reshape(GROUP_SLOTS, CHUNKS_IN[g][c]), 1, c, False)

    def hidden(g, c):
        gate = acc_g[g]
        hid[g] = (gate / (1.0 + jnp.exp(-gate)) * acc_u[g]).astype(BF)
        push(hid.at[g], hid_sib.at[g], ("hid", g), sibling)

    def down(g, c):
        width = CHUNKS_OUT[g][c]
        columns = pl.ds(out_at[g][c], width)
        once("wd")
        total = dot(hid[g], wd_own[:, columns])
        if c == 0:
            if g == 0:
                arrived(wd_sib, "wd")
            arrived(hid_sib.at[g], ("hid", g))
        total = total + dot(hid_sib[g], wd_sib[:, columns])
        blocks = total.astype(BF).reshape(PLANE, BLOCK, width)
        ret[g][c][0] = blocks[0]
        outb[g][c][...] = blocks[1:]
        for block in PLANE_ORDER:
            push(outb[g][c].at[block - 1], ret[g][c].at[block], ("rp", g, c), in_plane(block, -1))

    def combine(g, c):
        width = CHUNKS_OUT[g][c]
        arrived(ret[g][c].at[pl.ds(1, PLANE - 1)], ("rp", g, c))
        block = ret[g][c][...].reshape(GROUP_SLOTS, width)
        part = dot(w_hi[g], block) + dot(w_lo[g], block)
        if g == 0:
            own[:, pl.ds(out_at[g][c], width)] = part[0:ROWS]
        zsend[g][c][...] = part.astype(BF).reshape(PER, ROWS, width)
        for p in Z_ORDERS[g]:
            push(zsend[g][c].at[p], zrecv[g][c].at[p], ("rz", g, c), along_z(-GROUPS[g][p]))

    def finish(g, c):
        arrived(zrecv[g][c].at[far(g)], ("rz", g, c))
        columns = pl.ds(out_at[g][c], CHUNKS_OUT[g][c])
        total = own[:, columns] + jnp.sum(zrecv[g][c][far(g)].astype(F32), 0)
        if g == 0:
            own[:, columns] = total
        else:
            out[:, columns] = total.astype(BF)

    stages = {
        "T": tables, "S": select, "F": forward, "M": halves, "X": siblings,
        "H": hidden, "D": down, "C": combine, "N": finish,
    }
    for name, g, c in STEPS:
        stages[name](int(g), int(c))

    for ref, key in sent:
        whole(ref, key).wait_send()
    assert len(index) <= send_sem.shape[0]


def layer(tokens, expert_ids, gate_scores, w_gate, w_up, w_down):
    vmem = pltpu.VMEM
    ins = lambda *lead: [vmem((*lead, w), BF) for widths in CHUNKS_IN for w in widths]
    outs = lambda *lead: [vmem((*lead, w), BF) for widths in CHUNKS_OUT for w in widths]
    sems = 4 + 3 * len(sum(CHUNKS_IN, ())) + 2 * len(sum(CHUNKS_OUT, ()))
    scratch = (
        ins(PER, ROWS) + ins(PLANE - 1, BLOCK) + ins(PLANE, BLOCK) + ins(PLANE, BLOCK)
        + outs(PLANE - 1, BLOCK) + outs(PLANE, BLOCK) + outs(PER, ROWS) + outs(PER, ROWS)
        + [
            vmem((TOP, ROWS), jnp.int32),
            vmem((TOP, ROWS), F32),
            vmem((NZ, TOP, 128), BF),
            vmem((2, GROUP_SLOTS, GROUP_ROWS), BF),
            vmem((2, GROUP_ROWS, GROUP_SLOTS), BF),
            vmem((2, GROUP_ROWS, GROUP_SLOTS), BF),
            vmem((2, GROUP_SLOTS, HID), BF),
            vmem((2, GROUP_SLOTS, HID), BF),
            vmem((2, GROUP_SLOTS, HID), F32),
            vmem((2, GROUP_SLOTS, HID), F32),
            vmem((ROWS, HALF), F32),
            vmem((2, HALF, HID), BF),
            vmem((2, HALF, HID), BF),
            vmem((HID, HALF), BF),
            vmem((HID, HALF), BF),
            vmem((ROWS, HALF), BF),
            pltpu.SemaphoreType.DMA((8,)),
            pltpu.SemaphoreType.DMA((sems,)),
            pltpu.SemaphoreType.DMA((sems,)),
        ]
    )
    return pl.pallas_call(
        kernel,
        out_shape=jax.ShapeDtypeStruct((ROWS, HALF), BF),
        in_specs=[pl.BlockSpec(memory_space=pl.ANY)] * 6,
        out_specs=pl.BlockSpec(memory_space=pltpu.VMEM),
        scratch_shapes=scratch,
        compiler_params=pltpu.CompilerParams(
            collective_id=0, has_side_effects=True, vmem_limit_bytes=56 << 20
        ),
    )(tokens, expert_ids.T, gate_scores.T, w_gate, w_up, w_down)


def solution(mesh):
    in_specs = (
        P("expert", None),
        P("expert", None),
        P("expert", None),
        P("expert", None, "rep"),
        P("expert", None, "rep"),
        P("expert", "rep", None),
    )
    return jax.shard_map(layer, mesh=mesh, in_specs=in_specs, out_specs=P("expert", "rep"), check_vma=False)
```
